128 devices in a mesh: axial: 8 (over y, z_hi), azim: 16 (over z_lo, x, core).
Axes of the slice: x: 4, y: 4, z: 4 (z_hi: 2, z_lo: 2; z = z_hi * 2 + z_lo), core: 2. Of those that a mesh axis runs over, the one named last changes fastest.
Arguments:
- gas: float32 [13, 64, 512, 128], P(None, 'axial', 'azim'), may hold values from -6 to 6
- diffusivity: float32 [13], replicated, may hold values from 0.04 to 0.12
- swirl: float32 [64, 512, 128], P('axial', 'azim'), may hold values from 0.1 to 0.25
- drops: float32 [2048, 13, 128], P(('axial', 'azim')), may hold values from -6 to 6
- mass: float32 [2048, 128], P(('axial', 'azim')), may hold values from 0.2 to 5
- azim_weight: float32 [2048, 128], P(('axial', 'azim')), may hold values from 0 to 1
- cell_index: int32 [2048, 128], P(('axial', 'azim')), may hold values from 0 to 32767, as said below
- bin_rows: int32 [2048], P(('axial', 'azim')), may hold values from 0 to 128, as said below
- destination: int32 [2048, 1], P(('axial', 'azim')), may hold values from 0 to 15; in each aligned block of 16 rows (0 to 15, 16 to 31, ...) at most 2 rows name the same one
Outputs:
- gas_out: float32 [13, 64, 512, 128], P(None, 'axial', 'azim')
- moved_drops: float32 [4096, 13, 128], P(('axial', 'azim'))
- moved_rows: int32 [4096], P(('axial', 'azim'))
The draws below stay inside these ranges and needn't reach their ends.
Inputs may be any that keep to these rules, and one draw needn't show every extreme that they name: `bin_rows`: each bin holds 0 to 128 live rows, and some bin holds 128. `destination`: among the 16 bins of one device no sector is named more than 2 times. `cell_index`: some droplet lies in its block's first cell and some in its last.
All inputs are finite; a program needn't handle non-finite values.
Results may differ from the reference program's by a relative error of at most 0.0003.
Values sent between devices are 32-bit elements; how exact they have to be, the bound alone decides.
A program may use at most 192 MiB of HBM per device.

```python
import math
import jax
import jax.numpy as jnp
import numpy as np

NV = 13
CA = 8
CT = 32
CR = 128
NBIN = 16
BROWS = 128
SUBSTEPS = 4
CAP = 2
NX = 64
NT = 512
BINS = 2048
SLOTS = 4096
N_AXIAL = 8
N_AZIM = 16


def draw_bin_rows(key, part):
    key = jax.random.fold_in(key, 7)
    key_full, key_part, key_selection = jax.random.split(key, 3)
    devices = BINS // NBIN
    full_bins = jax.random.randint(key_full, (devices, 1), 0, NBIN + 1)
    partial_value = jax.random.randint(key_part, (devices, NBIN), 0, BROWS + 1)
    position = jnp.arange(NBIN)[None, :]
    counts = jnp.where(position < full_bins, BROWS, partial_value)
    selected_droplet_bin = jax.random.randint(key_selection, (), 0, devices)
    counts = counts.at[selected_droplet_bin, 0].set(BROWS)
    return counts.reshape(BINS).astype(jnp.int32)


def draw_cell_index(key, part):
    key = jax.random.fold_in(key, 11)
    key_a, key_t, key_r, key_coin, key_selection = jax.random.split(key, 5)
    shape = (BINS, BROWS)
    lengthwise_cell_index = jax.random.randint(key_a, shape, 0, CA)
    azim_cell = jax.random.randint(key_t, shape, 0, CT)
    radial_cell = jax.random.randint(key_r, shape, 0, CR)
    coin = jax.random.randint(key_coin, shape, 0, 4)
    azim_cell = jnp.where(coin < 3, CT - 1, azim_cell)
    index = ((lengthwise_cell_index * CT + azim_cell) * CR + radial_cell).reshape(BINS * BROWS)
    total = BINS * BROWS
    pick = jax.random.randint(key_selection, (), 0, total)
    index = index.at[pick].set(CA * CT * CR - 1)
    index = index.at[(pick + total // 2) % total].set(0)
    return index.reshape(shape).astype(jnp.int32)


def block_levels(rng, dims, cuts, smallest, high):
    level = 1.0
    for dim, shards_of in cuts:
        heights = jax.random.uniform(jax.random.fold_in(jax.random.fold_in(rng, 6), dim), (shards_of,), jnp.float32, smallest / len(cuts), high / len(cuts))
        level = level * jnp.repeat(jnp.exp(heights), dims[dim] // shards_of).reshape((-1,) + (1,) * (len(dims) - 1 - dim))
    return level


def assign_block(stream_key, own, number, rows, count, top, most, slope):
    order = jax.random.permutation(stream_key, count)
    packed, ordinary = portions_of(count, rows * top, most, slope, True), portions_of(count, rows * top, most, slope, False)
    places = jnp.arange(count)

    def named(tallies, rotation):
        used = int((tallies > 0).sum())
        fixed = max(1, used // 4)
        moved = fixed + (places - fixed + rotation * (used - fixed)) % max(1, count - fixed)
        return jnp.zeros((count,), jnp.int32).at[order[jnp.where(places < fixed, places, moved)]].set(jnp.asarray(tallies, jnp.int32))

    tallies = jnp.where(number % 4 == 0, named(packed, number // 4), named(ordinary, number - number // 4 - 1))
    mixed = jax.random.permutation(jax.random.fold_in(own, 3), count)
    source_of, sink = mixed[0:count // 2 * 2:2], mixed[1:count // 2 * 2:2]
    room = jnp.minimum(tallies[source_of] - 1, most - tallies[sink]) // 2
    room = jnp.where((source_of == order[0]) | (sink == order[0]) | (tallies[sink] == 0), 0, jnp.maximum(room, 0))
    moved = jax.random.randint(jax.random.fold_in(own, 4), (count // 2,), 0, 1 << 20) % (room + 1)
    tallies = tallies.at[source_of].add(-moved).at[sink].add(moved)
    labels = jnp.searchsorted(jnp.cumsum(tallies), jnp.arange(rows * top), side="right").astype(jnp.int32)
    grid = labels.reshape(top, rows).T
    grid = grid[jax.random.permutation(jax.random.fold_in(own, 1), rows)]
    rotation = jax.random.randint(jax.random.fold_in(own, 2), (rows, 1), 0, top)
    return jnp.take_along_axis(grid, (jnp.arange(top)[None, :] + rotation) % top, axis=1)


def portions_of(count, total, most, lean, full):
    portions = [(1 << 20) // math.isqrt(standing ** lean) + 1 for standing in range(1, count + 1)]
    largest = most if full else min(most, max(-(-total // count), total * portions[0] // sum(portions)))
    least = 1 if total - largest >= count - 1 else 0
    holding, surplus = [largest] + [least] * (count - 1), total - largest - least * (count - 1)
    while surplus > 0:
        candidates = [i for i in range(1, count) if holding[i] < largest] or [i for i in range(1, count) if holding[i] < most]
        whole, remaining = sum([portions[i] for i in candidates]), surplus
        for i in candidates:
            more = min(most - holding[i], max(1, remaining * portions[i] // whole), surplus)
            holding[i] = holding[i] + more
            surplus = surplus - more
    return np.array(holding)


def bell_draw(rng, shape, scale, reach, cuts=(), kind=jnp.bfloat16):
    array = jax.random.normal(rng, shape, jnp.float32) * scale
    if len(cuts) > 0:
        array = block_levels(rng, shape, cuts, -0.22, 0.18) * array
    return jnp.clip(array, min=-reach, max=reach).astype(kind)


def setup_inputs(seed: int = 0) -> dict:
    arg_keys = jax.random.split(jax.random.key(seed), 10)
    gas = bell_draw(arg_keys[0], (NV, NX, NT, CR), 1.0, 6.0, ((1, 8), (2, 16)), jnp.float32)
    diffusivity = jnp.clip(jnp.exp(jax.random.uniform(arg_keys[1], (NV,), jnp.float32, math.log(0.04), math.log(0.12))), 0.04, 0.12)
    swirl = jnp.clip(0.1 + 0.15 * jax.random.uniform(arg_keys[2], (NX, NT, CR), jnp.float32) ** block_levels(arg_keys[2], (NX, NT, CR), ((0, 8), (1, 16)), -0.2, 0.2), 0.1, 0.25)
    drops = bell_draw(arg_keys[3], (BINS, NV, BROWS), 1.0, 6.0, ((0, 128),), jnp.float32)
    mass = jnp.clip(jnp.exp(math.log(5.0) - 3.218876 * jax.random.uniform(arg_keys[4], (BINS, BROWS), jnp.float32) ** block_levels(arg_keys[4], (BINS, BROWS), ((0, 128),), -0.2, 0.2)), 0.2, 5.0)
    azim_weight = jnp.clip(1.0 * jax.random.uniform(arg_keys[5], (BINS, BROWS), jnp.float32) ** block_levels(arg_keys[5], (BINS, BROWS), ((0, 128),), -0.2, 0.2), 0.0, 1.0)
    cell_index = draw_cell_index(jax.random.fold_in(arg_keys[9], 71), 0)
    bin_rows = draw_bin_rows(jax.random.fold_in(arg_keys[9], 71), 0)
    destination_keys = jax.random.split(jax.random.fold_in(arg_keys[8], 1), BINS // NBIN)
    destination_turns = jax.random.permutation(jax.random.fold_in(arg_keys[8], 3), BINS // NBIN)
    destination = jax.vmap(lambda own, number: assign_block(jax.random.fold_in(arg_keys[8], 2), own, number, NBIN, N_AZIM, 1, CAP, 2))(destination_keys, destination_turns).reshape((BINS, 1))
    return dict(gas=gas, diffusivity=diffusivity, swirl=swirl, drops=drops, mass=mass, azim_weight=azim_weight, cell_index=cell_index, bin_rows=bin_rows, destination=destination)


source_load = 2.0


def reference(gas, diffusivity, swirl, drops, mass, azim_weight, cell_index, bin_rows, destination):
    nvar = gas.shape[0]
    devices = N_AXIAL * N_AZIM
    rows = jnp.arange(BROWS, dtype=jnp.int32)
    live = (rows[None, :] < bin_rows[:, None]).astype(jnp.float32)
    device = (jnp.arange(BINS, dtype=jnp.int32) // NBIN).astype(jnp.int32)
    axial_idx = device // N_AZIM
    azim_idx = device % N_AZIM
    a_loc = cell_index // (CT * CR)
    t_loc = (cell_index // CR) % CT
    r_loc = cell_index % CR
    glob_a = axial_idx[:, None] * CA + a_loc
    glob_t = azim_idx[:, None] * CT + t_loc
    glob_next = (glob_t + 1) % NT
    first = ((glob_a * NT + glob_t) * CR + r_loc).astype(jnp.int32)
    second = ((glob_a * NT + glob_next) * CR + r_loc).astype(jnp.int32)
    near = 1.0 - azim_weight
    diff = diffusivity[:, None, None, None]
    for step in range(SUBSTEPS):
        field = gas.reshape(nvar, -1)
        lower = jnp.moveaxis(jnp.take(field, first, axis=1), 0, 1)
        upper = jnp.moveaxis(jnp.take(field, second, axis=1), 0, 1)
        sample = near[:, None, :] * lower + azim_weight[:, None, :] * upper
        rate = 0.5 * mass / (1.0 + mass) * (1.0 + 0.5 * jnp.tanh(sample[:, 0, :])) * live
        transfer = rate[:, None, :] * (drops - sample)
        drops = drops - transfer
        part_low = jnp.moveaxis(source_load * near[:, None, :] * transfer, 1, 0)
        part_high = jnp.moveaxis(source_load * azim_weight[:, None, :] * transfer, 1, 0)
        source = jnp.zeros_like(field).at[:, first].add(part_low).at[:, second].add(part_high)
        source = source.reshape(gas.shape)
        halo_extended_field = jnp.pad(gas, ((0, 0), (1, 1), (0, 0), (1, 1)))
        behind = jnp.roll(gas, 1, axis=2)
        adjacent_neighbour_cells = behind + jnp.roll(gas, -1, axis=2)
        adjacent_neighbour_cells = adjacent_neighbour_cells + halo_extended_field[:, 2:, :, 1:-1] + halo_extended_field[:, :-2, :, 1:-1]
        adjacent_neighbour_cells = adjacent_neighbour_cells + halo_extended_field[:, 1:-1, :, 2:] + halo_extended_field[:, 1:-1, :, :-2]
        gas = gas + diff * (adjacent_neighbour_cells - 6.0 * gas) - swirl[None] * (gas - behind) + source
    target = destination[:, 0].reshape(devices, NBIN)
    order = jnp.arange(NBIN, dtype=jnp.int32)
    previous_gas_state = (target[:, :, None] == target[:, None, :]) & (order[None, None, :] < order[None, :, None])
    rank = jnp.sum(previous_gas_state.astype(jnp.int32), axis=2).reshape(BINS)
    slot = (((axial_idx * N_AZIM + destination[:, 0]) * N_AZIM + azim_idx) * CAP + rank).astype(jnp.int32)
    moved_drops = jnp.zeros((SLOTS, nvar, BROWS), jnp.float32).at[slot].set(drops * live[:, None, :])
    moved_rows = jnp.zeros((SLOTS,), jnp.int32).at[slot].set(bin_rows)
    return gas, moved_drops, moved_rows
```

```python
import functools

import jax
import jax.numpy as jnp
from jax import lax
from jax.experimental import pallas as pl
from jax.experimental.pallas import tpu as pltpu
from jax.sharding import PartitionSpec as P

MESH = pl.DeviceIdType.MESH
F32, BF16 = jnp.float32, jnp.bfloat16

SUBSTEPS = 4
CAP = 2
NV, CA, CT, CR = 13, 8, 32, 128
NBIN, BROWS = 16, 128
DROPLETS = NBIN * BROWS
LANES = CA * CR
MAIN = NV * CT
VROWS = 16
ROWS = 2 * MAIN + 2 * VROWS
CHUNK = 256

ORDER = (1, 2, 3, 4, 5, 6, 0, 7)
PLACE = {a: i for i, a in enumerate(ORDER)}
INNER, OUTER = (0, 768), (768, 256)


def lanes_of(a):
    return pl.ds(PLACE[a] * CR, CR)


def split(x):
    hi = x.astype(BF16)
    return hi, (x - hi.astype(F32)).astype(BF16)


def kernel(
    sectors, slabs,
    gas, diffusivity, swirl, drops, mass, azim_weight, cell_index, bin_rows, destination,
    gas_out, moved_out,
    G, F, R, RT, W, L, D, Q, T, OUT, DEP, AX, LOW, HIGH, DEPR, FIRST, LAST, PAY, GOT,
    load_sem, save_sem, ax_send, ax_recv, low_send, low_recv, high_send, high_recv, dep_send, dep_recv,
    pay_send, pay_recv,
):
    ax, az = lax.axis_index("axial"), lax.axis_index("azim")
    up_az, down_az = lax.rem(az + 1, sectors), lax.rem(az + sectors - 1, sectors)
    up_ax, down_ax = lax.rem(ax + 1, slabs), lax.rem(ax + slabs - 1, slabs)
    has_up, has_down = ax < slabs - 1, ax > 0
    parts = (OUTER, INNER)

    def load(a):
        return pltpu.make_async_copy(gas.at[:, a], G.at[0, :, :, lanes_of(a)], load_sem.at[a])

    def save(a):
        return pltpu.make_async_copy(
            G.at[SUBSTEPS % 2, :, :, lanes_of(a)], gas_out.at[:, a], save_sem.at[a]
        )

    def axial(src_up, src_down, s):
        upward = pltpu.make_async_remote_copy(
            src_up, AX.at[s, 0], ax_send.at[s, 0], ax_recv.at[s, 0],
            device_id=(up_ax, az), device_id_type=MESH,
        )
        downward = pltpu.make_async_remote_copy(
            src_down, AX.at[s, 1], ax_send.at[s, 1], ax_recv.at[s, 1],
            device_id=(down_ax, az), device_id_type=MESH,
        )
        return upward, downward

    def axial_of(s):
        buf = lax.rem(s, 2)
        return axial(G.at[buf, :, :, lanes_of(CA - 1)], G.at[buf, :, :, lanes_of(0)], s)

    def axial_start(copies):
        upward, downward = copies

        @pl.when(has_up)
        def _():
            upward.start()

        @pl.when(has_down)
        def _():
            downward.start()

    def axial_wait_send(copies):
        upward, downward = copies

        @pl.when(has_up)
        def _():
            upward.wait_send()

        @pl.when(has_down)
        def _():
            downward.wait_send()

    def axial_wait_recv(copies):
        upward, downward = copies

        @pl.when(has_down)
        def _():
            upward.wait_recv()

        @pl.when(has_up)
        def _():
            downward.wait_recv()

    def azim_of(s, p):
        lanes = pl.ds(*parts[p])
        low = pltpu.make_async_remote_copy(
            LAST.at[:, lanes], LOW.at[s, :, lanes], low_send.at[s, p], low_recv.at[s, p],
            device_id=(ax, up_az), device_id_type=MESH,
        )
        high = pltpu.make_async_remote_copy(
            FIRST.at[:, lanes], HIGH.at[s, :, lanes], high_send.at[s, p], high_recv.at[s, p],
            device_id=(ax, down_az), device_id_type=MESH,
        )
        return low, high

    def dep_of(s, p):
        lanes = pl.ds(*parts[p])
        return pltpu.make_async_remote_copy(
            DEP.at[pl.ds(MAIN, VROWS), lanes], DEPR.at[s, :, lanes], dep_send.at[s, p], dep_recv.at[s, p],
            device_id=(ax, up_az), device_id_type=MESH,
        )

    def pay_of(j):
        there = lax.rem(az + j, sectors)
        return pltpu.make_async_remote_copy(
            PAY.at[pl.ds(there * CAP, CAP)], GOT.at[pl.ds(az * CAP, CAP)], pay_send.at[j], pay_recv.at[j],
            device_id=(ax, there), device_id_type=MESH,
        )

    for a in (0, 7, 1, 2, 3, 4, 5, 6):
        load(a).start()
    barrier = pltpu.get_barrier_semaphore()
    for j in range(1, sectors):
        pl.semaphore_signal(
            barrier, inc=1, device_id=(ax, lax.rem(az + j, sectors)), device_id_type=MESH
        )
    for other in (up_ax, down_ax):
        pl.semaphore_signal(barrier, inc=1, device_id=(other, az), device_id_type=MESH)
    pl.semaphore_wait(barrier, sectors + 1)
    axial_start(axial(gas.at[:, CA - 1], gas.at[:, 0], 0))

    @pl.when(jnp.logical_not(has_down))
    def _():
        AX[:, 0] = jnp.zeros((SUBSTEPS, NV, CT, CR), F32)

    @pl.when(jnp.logical_not(has_up))
    def _():
        AX[:, 1] = jnp.zeros((SUBSTEPS, NV, CT, CR), F32)

    FIRST[...] = jnp.zeros((VROWS, LANES), F32)
    LAST[...] = jnp.zeros((VROWS, LANES), F32)
    for a in range(CA):
        load(a).wait()
    for v in range(NV):
        FIRST[v : v + 1, :] = G[0, v, 0:1, :]
        LAST[v : v + 1, :] = G[0, v, CT - 1 : CT, :]
    for p in range(2):
        for copy in azim_of(0, p):
            copy.start()

    cell = cell_index[...]
    layer = cell // (CT * CR)
    place = jnp.where(layer == 0, CA - 2, jnp.where(layer == CA - 1, CA - 1, layer - 1))
    key = place * CR + cell % CR
    key_row = jnp.concatenate([key[b : b + 1] for b in range(NBIN)], axis=1)
    cell_row = jnp.concatenate([cell[b : b + 1] for b in range(NBIN)], axis=1)
    weight = jnp.concatenate([azim_weight[b : b + 1, :] for b in range(NBIN)], axis=1)
    m = mass[...]
    lane = lax.broadcasted_iota(jnp.int32, (1, BROWS), 1)
    half = 0.5 * m / (1.0 + m)
    live = [(lane < bin_rows[b]).astype(F32) for b in range(NBIN)]
    Q[0:1, :] = jnp.concatenate([half[b : b + 1] * live[b] for b in range(NBIN)], axis=1)
    Q[1:2, :] = jnp.where(key_row >= OUTER[0], 1.0, 0.0)
    azim_row = cell_row // CR % CT
    for t0 in range(0, 40, 8):
        t = lax.broadcasted_iota(jnp.int32, (8, DROPLETS), 0) + t0
        W[t0 : t0 + 8, :] = jnp.where(t == azim_row, 1.0 - weight, 0.0) + jnp.where(
            t == azim_row + 1, weight, 0.0
        )
    D[...] = jnp.zeros((VROWS, DROPLETS), F32)
    T[...] = jnp.zeros((VROWS, DROPLETS), F32)
    for b in range(NBIN):
        D[0:NV, b * BROWS : (b + 1) * BROWS] = drops[b]
    for k in range(0, LANES, 16):
        rows = lax.broadcasted_iota(jnp.int32, (16, DROPLETS), 0) + k
        R[k : k + 16, :] = jnp.where(rows == key_row, 1.0, 0.0).astype(BF16)
    key_column = jnp.transpose(key.astype(F32)).astype(jnp.int32)
    for b in range(NBIN):
        for k in range(0, LANES, CR):
            columns = lax.broadcasted_iota(jnp.int32, (BROWS, CR), 1) + k
            RT[b * BROWS : (b + 1) * BROWS, k : k + CR] = jnp.where(
                columns == key_column[:, b : b + 1], 1.0, 0.0
            ).astype(BF16)
    for v in range(NV):
        hi, lo = split(G[0, v])
        F[v * CT : (v + 1) * CT, :] = hi
        F[MAIN + v * CT : MAIN + (v + 1) * CT, :] = lo

    def droplets(s, p):
        start, width = parts[p]
        lanes = pl.ds(start, width)
        for copy in azim_of(s, p)[1:]:
            copy.wait_recv()
        hi, lo = split(HIGH[s, :, lanes])
        F[2 * MAIN : 2 * MAIN + VROWS, lanes] = hi
        F[2 * MAIN + VROWS : ROWS, lanes] = lo
        for c in range(0, DROPLETS, CHUNK):
            ps = pl.ds(c, CHUNK)
            x = jnp.dot(F[:, lanes], R[lanes, ps], preferred_element_type=F32)
            near = (x[:MAIN] + x[MAIN : 2 * MAIN]).reshape(NV, CT, CHUNK)
            far = x[2 * MAIN : 2 * MAIN + VROWS] + x[2 * MAIN + VROWS :]
            w, w_far = W[0:CT, ps], W[CT : CT + 1, ps]
            sample = jnp.sum(near * w[None], axis=1) + w_far * far[0:NV]
            rate = Q[0:1, ps] * (1.0 + 0.5 * jnp.tanh(sample[0:1]))
            carried = D[0:NV, ps]
            transfer = rate * (carried - sample)
            if p == 0:
                OUT[0:NV, ps] = transfer
            else:
                D[0:NV, ps] = carried - jnp.where(Q[1:2, ps] > 0.0, OUT[0:NV, ps], transfer)
            T[0:NV, ps] = 2.0 * transfer
            for v in range(NV):
                hi, lo = split(w * T[v : v + 1, ps])
                L[v * CT : (v + 1) * CT, ps] = hi
                L[MAIN + v * CT : MAIN + (v + 1) * CT, ps] = lo
            hi, lo = split(w_far * T[:, ps])
            L[2 * MAIN : 2 * MAIN + VROWS, ps] = hi
            L[2 * MAIN + VROWS : ROWS, ps] = lo

        if p == 0:
            @pl.when(s > 0)
            def _():
                for q in range(2):
                    dep_of(s - 1, q).wait_send()

        for k in range(start, start + width, CHUNK):
            ks = pl.ds(k, CHUNK)
            x = jnp.dot(L[...], RT[:, ks], preferred_element_type=F32)
            DEP[0:MAIN, ks] = x[:MAIN] + x[MAIN : 2 * MAIN]
            DEP[MAIN : MAIN + VROWS, ks] = x[2 * MAIN : 2 * MAIN + VROWS] + x[2 * MAIN + VROWS :]
        dep_of(s, p).start()

    def stencil(s, p):
        now = lax.rem(s, 2)
        later = 1 - now
        azim_of(s, p)[0].wait_recv()
        dep_of(s, p).wait_recv()
        row = lax.broadcasted_iota(jnp.int32, (CT, CR), 0)
        column = lax.broadcasted_iota(jnp.int32, (CT, CR), 1)
        for v in range(NV):
            d = diffusivity[v]
            one = pl.ds(v, 1)
            for a in ((0, CA - 1) if p == 0 else range(1, CA - 1)):
                here = lanes_of(a)
                c = G[now, v, :, here]
                below = AX[s, 0, v] if a == 0 else G[now, v, :, lanes_of(a - 1)]
                above = AX[s, 1, v] if a == CA - 1 else G[now, v, :, lanes_of(a + 1)]
                behind = jnp.where(row == 0, LOW[s, one, here], pltpu.roll(c, 1, 0))
                ahead = jnp.where(row == CT - 1, HIGH[s, one, here], pltpu.roll(c, CT - 1, 0))
                inward = jnp.where(column == 0, 0.0, pltpu.roll(c, 1, 1))
                outward = jnp.where(column == CR - 1, 0.0, pltpu.roll(c, CR - 1, 1))
                around = behind + ahead + above + below + outward + inward
                source = DEP[v * CT : (v + 1) * CT, here]
                source = source + jnp.where(row == 0, DEPR[s, one, here], 0.0)
                new = c + d * (around - 6.0 * c) - swirl[a] * (c - behind) + source
                G[later, v, :, here] = new
                hi, lo = split(new)
                F[v * CT : (v + 1) * CT, here] = hi
                F[MAIN + v * CT : MAIN + (v + 1) * CT, here] = lo
                FIRST[one, here] = new[0:1]
                LAST[one, here] = new[CT - 1 : CT]

    def send_bins():
        slot = []
        for b in range(NBIN):
            rank = jnp.int32(0)
            for e in range(b):
                rank = rank + jnp.where(destination[e, 0] == destination[b, 0], 1, 0)
            slot.append(destination[b, 0] * CAP + rank)
        row = lax.broadcasted_iota(jnp.int32, (VROWS, BROWS), 0)
        pay = [
            jnp.where(
                row == NV, bin_rows[b].astype(F32), D[:, b * BROWS : (b + 1) * BROWS] * live[b]
            )
            for b in range(NBIN)
        ]
        for k in range(sectors * CAP):
            total = jnp.zeros((VROWS, BROWS), F32)
            for b in range(NBIN):
                total = total + jnp.where(slot[b] == k, 1.0, 0.0) * pay[b]
            PAY[k] = total
        for j in range(1, sectors):
            pay_of(j).start()
        mine = pl.ds(az * CAP, CAP)
        GOT[mine] = PAY[mine]

    @pl.loop(0, SUBSTEPS)
    def _(s):
        droplets(s, 0)
        droplets(s, 1)

        @pl.when(s == SUBSTEPS - 1)
        def _():
            send_bins()

        copies = axial_of(s)
        axial_wait_send(copies)
        for p in range(2):
            for copy in azim_of(s, p):
                copy.wait_send()
        axial_wait_recv(copies)
        stencil(s, 0)

        @pl.when(s < SUBSTEPS - 1)
        def _():
            axial_start(axial_of(s + 1))
            for copy in azim_of(s + 1, 0):
                copy.start()

        @pl.when(s == SUBSTEPS - 1)
        def _():
            for a in (0, CA - 1):
                save(a).start()

        stencil(s, 1)

        @pl.when(s < SUBSTEPS - 1)
        def _():
            for copy in azim_of(s + 1, 1):
                copy.start()

    for a in range(1, CA - 1):
        save(a).start()
    for q in range(2):
        dep_of(SUBSTEPS - 1, q).wait_send()
    for j in range(1, sectors):
        pay_of(j).wait()
    moved_out[...] = GOT[...]
    for a in range(CA):
        save(a).wait()


def body(gas, diffusivity, swirl, drops, mass, azim_weight, cell_index, bin_rows, destination):
    sectors, slabs = lax.axis_size("azim"), lax.axis_size("axial")
    anywhere = pl.BlockSpec(memory_space=pl.ANY)
    vmem = pl.BlockSpec(memory_space=pltpu.VMEM)
    smem = pl.BlockSpec(memory_space=pltpu.SMEM)
    sem = pltpu.SemaphoreType.DMA
    gas_out, moved = pl.pallas_call(
        functools.partial(kernel, sectors, slabs),
        out_shape=(
            jax.ShapeDtypeStruct((NV, CA, CT, CR), F32),
            jax.ShapeDtypeStruct((sectors * CAP, VROWS, BROWS), F32),
        ),
        in_specs=[anywhere, smem, vmem, vmem, vmem, vmem, vmem, smem, smem],
        out_specs=(anywhere, vmem),
        scratch_shapes=[
            pltpu.VMEM((2, NV, CT, LANES), F32),
            pltpu.VMEM((ROWS, LANES), BF16),
            pltpu.VMEM((LANES, DROPLETS), BF16),
            pltpu.VMEM((DROPLETS, LANES), BF16),
            pltpu.VMEM((40, DROPLETS), F32),
            pltpu.VMEM((ROWS, DROPLETS), BF16),
            pltpu.VMEM((VROWS, DROPLETS), F32),
            pltpu.VMEM((8, DROPLETS), F32),
            pltpu.VMEM((VROWS, DROPLETS), F32),
            pltpu.VMEM((VROWS, DROPLETS), F32),
            pltpu.VMEM((MAIN + VROWS, LANES), F32),
            pltpu.VMEM((SUBSTEPS, 2, NV, CT, CR), F32),
            pltpu.VMEM((SUBSTEPS, VROWS, LANES), F32),
            pltpu.VMEM((SUBSTEPS, VROWS, LANES), F32),
            pltpu.VMEM((SUBSTEPS, VROWS, LANES), F32),
            pltpu.VMEM((VROWS, LANES), F32),
            pltpu.VMEM((VROWS, LANES), F32),
            pltpu.VMEM((sectors * CAP, VROWS, BROWS), F32),
            pltpu.VMEM((sectors * CAP, VROWS, BROWS), F32),
            sem((CA,)), sem((CA,)),
            sem((SUBSTEPS, 2)), sem((SUBSTEPS, 2)),
            sem((SUBSTEPS, 2)), sem((SUBSTEPS, 2)),
            sem((SUBSTEPS, 2)), sem((SUBSTEPS, 2)),
            sem((SUBSTEPS, 2)), sem((SUBSTEPS, 2)),
            sem((sectors,)), sem((sectors,)),
        ],
        compiler_params=pltpu.CompilerParams(
            collective_id=0, has_side_effects=True, vmem_limit_bytes=48 << 20
        ),
    )(gas, diffusivity, swirl, drops, mass, azim_weight, cell_index, bin_rows, destination)
    return gas_out, moved[:, :NV], moved[:, NV, 0].astype(jnp.int32)


def solution(mesh):
    return jax.shard_map(
        body,
        mesh=mesh,
        in_specs=(
            P(None, "axial", "azim", None),
            P(),
            P("axial", "azim", None),
            P(("axial", "azim"), None, None),
            P(("axial", "azim"), None),
            P(("axial", "azim"), None),
            P(("axial", "azim"), None),
            P(("axial", "azim")),
            P(("axial", "azim"), None),
        ),
        out_specs=(
            P(None, "axial", "azim", None),
            P(("axial", "azim"), None, None),
            P(("axial", "azim")),
        ),
        check_vma=False,
    )
```

```python
import functools

import jax
import jax.numpy as jnp
from jax import lax
from jax.experimental import pallas as pl
from jax.experimental.pallas import tpu as pltpu
from jax.sharding import PartitionSpec as P

MESH = pl.DeviceIdType.MESH
F32, BF16 = jnp.float32, jnp.bfloat16

SUBSTEPS = 4
CAP = 2
NV, CA, CT, CR = 13, 8, 32, 128
NBIN, BROWS = 16, 128
DROPLETS = NBIN * BROWS
LANES = CA * CR
MAIN = NV * CT
VROWS = 16
ROWS = 2 * MAIN + 2 * VROWS
HALF = CT // 2
CHUNK = 256

ORDER = (1, 2, 3, 4, 5, 6, 0, 7)
PLACE = {a: i for i, a in enumerate(ORDER)}
PARTS = ((768, 256, (0, 7)), (0, 512, (1, 2, 3, 4)), (512, 256, (5, 6)))
GROUPS = ((0, 5), (5, 4), (9, 4))


def lanes_of(a):
    return pl.ds(PLACE[a] * CR, CR)


def split(x):
    hi = x.astype(BF16)
    return hi, (x - hi.astype(F32)).astype(BF16)


def kernel(
    sectors, slabs,
    gas, diffusivity, swirl, drops, mass, azim_weight, cell_index, bin_rows, destination,
    gas_out, moved_out, rows_out,
    G, F, S, R, WHERE, W, L, D, Q, T, OUT, DEP, AX, LOW, HIGH, DEPR, FIRST, LAST, PAY, GOT, BINS, SW, MASS, WEIGHT, CELL, DROPS, FROM,
    small_sem, save_sem, ax_send, ax_recv, low_send, low_recv, high_send, high_recv, dep_send, dep_recv,
    pay_send, pay_recv,
):
    ax, az = lax.axis_index("axial"), lax.axis_index("azim")
    up_az, down_az = lax.rem(az + 1, sectors), lax.rem(az + sectors - 1, sectors)
    up_ax, down_ax = lax.rem(ax + 1, slabs), lax.rem(ax + slabs - 1, slabs)
    has_up, has_down = ax < slabs - 1, ax > 0

    small = [
        pltpu.make_async_copy(src, dst, small_sem.at[i])
        for i, (src, dst) in enumerate(
            ((mass, MASS), (azim_weight, WEIGHT), (cell_index, CELL), (drops, DROPS), (swirl, SW), (gas, G.at[0]))
        )
    ]

    def axial_of(s, g, layer):
        v0, count = GROUPS[g]
        vs = pl.ds(v0, count)
        upward = pltpu.make_async_remote_copy(
            layer(vs, CA - 1), AX.at[s, 0, vs], ax_send.at[s, 0, g], ax_recv.at[s, 0, g],
            device_id=(up_ax, az), device_id_type=MESH,
        )
        downward = pltpu.make_async_remote_copy(
            layer(vs, 0), AX.at[s, 1, vs], ax_send.at[s, 1, g], ax_recv.at[s, 1, g],
            device_id=(down_ax, az), device_id_type=MESH,
        )
        return upward, downward

    def both(first, first_do, second, second_do):
        @pl.when(first)
        def _():
            first_do()

        @pl.when(second)
        def _():
            second_do()

    def azim_of(s, p):
        lanes = pl.ds(*PARTS[p][:2])
        low = pltpu.make_async_remote_copy(
            LAST.at[:, lanes], LOW.at[s, :, lanes], low_send.at[s, p], low_recv.at[s, p],
            device_id=(ax, up_az), device_id_type=MESH,
        )
        high = pltpu.make_async_remote_copy(
            FIRST.at[:, lanes], HIGH.at[s, :, lanes], high_send.at[s, p], high_recv.at[s, p],
            device_id=(ax, down_az), device_id_type=MESH,
        )
        return low, high

    def dep_of(s, p):
        lanes = pl.ds(*PARTS[p][:2])
        return pltpu.make_async_remote_copy(
            DEP.at[pl.ds(MAIN, VROWS), lanes], DEPR.at[s, :, lanes], dep_send.at[s, p], dep_recv.at[s, p],
            device_id=(ax, up_az), device_id_type=MESH,
        )

    def pay_of(j):
        there = lax.rem(az + j, sectors)
        return pltpu.make_async_remote_copy(
            PAY.at[pl.ds(there * CAP, CAP)], GOT.at[pl.ds(az * CAP, CAP)], pay_send.at[j], pay_recv.at[j],
            device_id=(ax, there), device_id_type=MESH,
        )

    for copy in small:
        copy.start()
    D[...] = jnp.zeros((VROWS, DROPLETS), F32)
    barrier = pltpu.get_barrier_semaphore()
    for j in range(1, sectors):
        pl.semaphore_signal(
            barrier, inc=1, device_id=(ax, lax.rem(az + j, sectors)), device_id_type=MESH
        )
    for other in (up_ax, down_ax):
        pl.semaphore_signal(barrier, inc=1, device_id=(other, az), device_id_type=MESH)

    @pl.when(jnp.logical_not(has_down))
    def _():
        AX[:, 0] = jnp.zeros((SUBSTEPS, NV, CT, CR), F32)

    @pl.when(jnp.logical_not(has_up))
    def _():
        AX[:, 1] = jnp.zeros((SUBSTEPS, NV, CT, CR), F32)

    FIRST[...] = jnp.zeros((VROWS, LANES), F32)
    LAST[...] = jnp.zeros((VROWS, LANES), F32)
    T[...] = jnp.zeros((VROWS, DROPLETS), F32)
    BINS[0] = jnp.zeros((VROWS, BROWS), F32)
    slot = []
    for b in range(NBIN):
        rank = jnp.int32(0)
        for e in range(b):
            rank = rank + jnp.where(destination[e] == destination[b], 1, 0)
        slot.append(destination[b] * CAP + rank)
    for k in range(sectors * CAP):
        source = jnp.int32(0)
        for b in range(NBIN):
            source = source + jnp.where(slot[b] == k, b + 1, 0)
        FROM[k] = source

    for copy in small[:4]:
        copy.wait()
    cell = CELL[...]
    layer = cell // (CT * CR)
    place = jnp.where(layer == 0, CA - 2, jnp.where(layer == CA - 1, CA - 1, layer - 1))
    key = place * CR + cell % CR
    key_row = jnp.concatenate([key[b : b + 1] for b in range(NBIN)], axis=1)
    cell_row = jnp.concatenate([cell[b : b + 1] for b in range(NBIN)], axis=1)
    weight = jnp.concatenate([WEIGHT[b : b + 1, :] for b in range(NBIN)], axis=1)
    m = MASS[...]
    lane = lax.broadcasted_iota(jnp.int32, (1, BROWS), 1)
    half = 0.5 * m / (1.0 + m)
    live = [(lane < bin_rows[b]).astype(F32) for b in range(NBIN)]
    Q[0:1, :] = jnp.concatenate([half[b : b + 1] * live[b] for b in range(NBIN)], axis=1)
    for q in range(2):
        first, count, _ = PARTS[q]
        Q[q + 1 : q + 2, :] = jnp.where(
            key_row >= first, jnp.where(key_row < first + count, 1.0, 0.0), 0.0
        )
    azim_row = cell_row // CR % CT
    WHERE[0:1, :] = cell_row % CR
    WHERE[1:2, :] = cell_row // (CT * CR)
    for t0 in range(0, 40, 8):
        t = lax.broadcasted_iota(jnp.int32, (8, DROPLETS), 0) + t0
        W[t0 : t0 + 8, :] = jnp.where(t == azim_row, 1.0 - weight, 0.0) + jnp.where(
            t == azim_row + 1, weight, 0.0
        )

    @pl.loop(0, LANES // 16)
    def _(k):
        for c in range(0, DROPLETS, 4 * CHUNK):
            rows = lax.broadcasted_iota(jnp.int32, (16, 4 * CHUNK), 0) + k * 16
            R[pl.ds(pl.multiple_of(k * 16, 16), 16), c : c + 4 * CHUNK] = jnp.where(
                rows == key_row[:, c : c + 4 * CHUNK], 1.0, 0.0
            ).astype(BF16)

    pl.semaphore_wait(barrier, sectors + 1)
    for g in range(len(GROUPS)):
        upward, downward = axial_of(0, g, lambda vs, a: gas.at[vs, a])
        both(has_up, upward.start, has_down, downward.start)
    for copy in small[4:]:
        copy.wait()
    for v in range(NV):
        for a in range(CA):
            FIRST[v : v + 1, lanes_of(a)] = G[0, v, a, 0:1, :]
            LAST[v : v + 1, lanes_of(a)] = G[0, v, a, CT - 1 : CT, :]
    for p in range(len(PARTS)):
        for copy in azim_of(0, p):
            copy.start()
    for v in range(NV):
        for a in range(CA):
            hi, lo = split(G[0, v, a])
            F[v * CT : (v + 1) * CT, lanes_of(a)] = hi
            F[MAIN + v * CT : MAIN + (v + 1) * CT, lanes_of(a)] = lo
    for v in range(NV):
        for b in range(NBIN):
            D[v : v + 1, b * BROWS : (b + 1) * BROWS] = DROPS[v, b : b + 1, :]

    def gather(p):
        lanes = pl.ds(*PARTS[p][:2])
        for c in range(0, DROPLETS, CHUNK):
            ps = pl.ds(c, CHUNK)
            x = jnp.dot(F[:, lanes], R[lanes, ps], preferred_element_type=F32)
            near = (x[:MAIN] + x[MAIN:]).reshape(NV, CT, CHUNK)
            S[p, 0:NV, ps] = jnp.sum(near * W[0:CT, ps][None], axis=1)

    def finish(s, p):
        start, width, layers = PARTS[p]
        azim_of(s, p)[1].wait_recv()
        for c in range(0, DROPLETS, CHUNK):
            ps = pl.ds(c, CHUNK)
            far = []
            for e in range(c, c + CHUNK, BROWS):
                es = pl.ds(e, BROWS)
                at = jnp.broadcast_to(WHERE[0:1, es], (8, BROWS))
                tops = []
                for top in (0, 8):
                    total = jnp.zeros((8, BROWS), F32)
                    for a in layers:
                        value = jnp.take_along_axis(
                            HIGH[s, top : top + 8, lanes_of(a)], at, axis=1, mode="promise_in_bounds"
                        )
                        total = total + jnp.where(WHERE[1:2, es] == a, value, 0.0)
                    tops.append(total)
                far.append(jnp.concatenate(tops, axis=0))
            far = jnp.concatenate(far, axis=1)
            w, w_far = W[0:CT, ps], W[CT : CT + 1, ps]
            sample = S[p, 0:NV, ps] + w_far * far[0:NV]
            rate = Q[0:1, ps] * (1.0 + 0.5 * jnp.tanh(sample[0:1]))
            carried = D[0:NV, ps]
            transfer = rate * (carried - sample)
            if p == 0:
                OUT[0:NV, ps] = transfer
            elif p == 1:
                OUT[0:NV, ps] = jnp.where(Q[1:2, ps] > 0.0, OUT[0:NV, ps], transfer)
            else:
                D[0:NV, ps] = carried - jnp.where(
                    Q[1:2, ps] + Q[2:3, ps] > 0.0, OUT[0:NV, ps], transfer
                )
            twice = 2.0 * transfer
            T[0:NV, ps] = twice
            for v in range(NV):
                hi, lo = split(w * twice[v : v + 1])
                L[v * CT : (v + 1) * CT, ps] = hi
                L[MAIN + v * CT : MAIN + (v + 1) * CT, ps] = lo
            hi, lo = split(w_far * T[:, ps])
            L[2 * MAIN : 2 * MAIN + VROWS, ps] = hi
            L[2 * MAIN + VROWS : ROWS, ps] = lo

        if p == 0:
            @pl.when(s > 0)
            def _():
                for q in range(len(PARTS)):
                    dep_of(s - 1, q).wait_send()

        for k in range(start, start + width, CHUNK):
            ks = pl.ds(k, CHUNK)
            x = lax.dot_general(
                L[...], R[ks, :], (((1,), (1,)), ((), ())), preferred_element_type=F32
            )
            DEP[0:MAIN, ks] = x[:MAIN] + x[MAIN : 2 * MAIN]
            DEP[MAIN : MAIN + VROWS, ks] = x[2 * MAIN : 2 * MAIN + VROWS] + x[2 * MAIN + VROWS :]
        dep_of(s, p).start()

    def stencil(s, now, p, halves=(0, 1), vs=(0, NV)):
        later = 1 - now
        sub = lax.broadcasted_iota(jnp.int32, (8, CR), 0)
        column = lax.broadcasted_iota(jnp.int32, (8, CR), 1)
        for v in range(vs[0], vs[0] + vs[1]):
            d = diffusivity[v]
            own = 1.0 - 6.0 * d
            one = pl.ds(v, 1)
            for a in PARTS[p][2]:
                here = lanes_of(a)
                tiles = [G[now, v, a, i * 8 : i * 8 + 8] for i in range(CT // 8)]
                for half in halves:
                    out = []
                    for i in (2 * half, 2 * half + 1):
                        rows = pl.ds(i * 8, 8)
                        c = tiles[i]
                        first = LOW[s, one, here] if i == 0 else pltpu.roll(tiles[i - 1], 1, 0)
                        behind = jnp.where(sub == 0, first, pltpu.roll(c, 1, 0))
                        last = HIGH[s, one, here] if i == 3 else pltpu.roll(tiles[i + 1], 7, 0)
                        ahead = jnp.where(sub == 7, last, pltpu.roll(c, 7, 0))
                        below = AX[s, 0, v, rows] if a == 0 else G[now, v, a - 1, rows]
                        above = AX[s, 1, v, rows] if a == CA - 1 else G[now, v, a + 1, rows]
                        inward = jnp.where(column == 0, 0.0, pltpu.roll(c, 1, 1))
                        outward = jnp.where(column == CR - 1, 0.0, pltpu.roll(c, CR - 1, 1))
                        around = (behind + ahead) + (above + below) + (outward + inward)
                        new = (own * c + d * around) + (SW[a, rows] * (behind - c))
                        new = new + DEP[pl.ds(v * CT + i * 8, 8), here]
                        if i == 0:
                            new = new + jnp.where(sub == 0, DEPR[s, one, here], 0.0)
                            FIRST[one, here] = new[0:1]
                        if i == 3:
                            LAST[one, here] = new[7:8]
                        G[later, v, a, rows] = new
                        out.append(new)
                    hi, lo = split(jnp.concatenate(out, axis=0))
                    at = v * CT + half * 16
                    F[at : at + 16, here] = hi
                    F[MAIN + at : MAIN + at + 16, here] = lo

    def send_bins():
        row = lax.broadcasted_iota(jnp.int32, (VROWS, BROWS), 0)
        for b in range(NBIN):
            alive = (lane < bin_rows[b]).astype(F32)
            BINS[b + 1] = jnp.where(
                row == NV, bin_rows[b].astype(F32), D[:, b * BROWS : (b + 1) * BROWS] * alive
            )
        for k in range(sectors * CAP):
            PAY[k] = BINS[FROM[k]]
        for j in range(1, sectors):
            pay_of(j).start()
        mine = pl.ds(az * CAP, CAP)
        GOT[mine] = PAY[mine]

    def save(a):
        return pltpu.make_async_copy(G.at[SUBSTEPS % 2, :, a], gas_out.at[:, a], save_sem.at[a])

    gather(0)
    gather(1)

    def substep(s, now):
        further = s < SUBSTEPS - 1

        def when_further(do):
            if now == 0:
                do()
            else:
                pl.when(further)(do)

        finish(s, 0)
        finish(s, 1)
        gather(2)
        finish(s, 2)
        if now == 1:
            pl.when(jnp.logical_not(further))(send_bins)
        for p in range(len(PARTS)):
            low, high = azim_of(s, p)
            low.wait_send()
            high.wait_send()
            low.wait_recv()
        dep_of(s, 0).wait_recv()
        for g in range(len(GROUPS)):
            upward, downward = axial_of(s, g, lambda vs, a: G.at[now, vs, a])
            both(has_up, upward.wait_send, has_down, downward.wait_send)
            both(has_down, upward.wait_recv, has_up, downward.wait_recv)
            stencil(s, now, 0, vs=GROUPS[g])

            @when_further
            def _():
                upward, downward = axial_of(s + 1, g, lambda vs, a: G.at[1 - now, vs, a])
                both(has_up, upward.start, has_down, downward.start)

        @when_further
        def _():
            for copy in azim_of(s + 1, 0):
                copy.start()

        dep_of(s, 1).wait_recv()
        stencil(s, now, 1)

        @when_further
        def _():
            for copy in azim_of(s + 1, 1):
                copy.start()

        stencil(s, now, 2, (1,))

        @when_further
        def _():
            gather(0)
            gather(1)

        dep_of(s, 2).wait_recv()
        stencil(s, now, 2, (0,))

        @when_further
        def _():
            for copy in azim_of(s + 1, 2):
                copy.start()

    @pl.loop(0, SUBSTEPS // 2)
    def _(i):
        substep(2 * i, 0)
        substep(2 * i + 1, 1)

    for a in range(CA):
        save(a).start()
    for q in range(len(PARTS)):
        dep_of(SUBSTEPS - 1, q).wait_send()
    for j in range(1, sectors):
        pay_of(j).wait()
    lines = jnp.concatenate([GOT[k, NV : NV + 1, :] for k in range(sectors * CAP)], axis=0)
    at = lax.broadcasted_iota(jnp.int32, lines.shape, 0)
    column = lax.broadcasted_iota(jnp.int32, lines.shape, 1)
    counts = jnp.sum(jnp.where(at == column, lines, 0.0), axis=0)
    rows_out[...] = counts[: sectors * CAP].astype(jnp.int32)
    for k in range(sectors * CAP):
        for v in range(NV):
            moved_out[v, k : k + 1, :] = GOT[k, v : v + 1, :]
    for a in range(CA):
        save(a).wait()


def body(gas, diffusivity, swirl, drops, mass, azim_weight, cell_index, bin_rows, destination):
    sectors, slabs = lax.axis_size("azim"), lax.axis_size("axial")
    hbm = pl.BlockSpec(memory_space=pltpu.HBM)
    vmem = pl.BlockSpec(memory_space=pltpu.VMEM)
    smem = pl.BlockSpec(memory_space=pltpu.SMEM)
    sem = pltpu.SemaphoreType.DMA
    parts = len(PARTS)
    slots = sectors * CAP
    gas, moved, rows = pl.pallas_call(
        functools.partial(kernel, sectors, slabs),
        out_shape=(
            jax.ShapeDtypeStruct((NV, CA, CT, CR), F32),
            jax.ShapeDtypeStruct((NV, slots, BROWS), F32),
            jax.ShapeDtypeStruct((slots,), jnp.int32),
        ),
        in_specs=[hbm, smem, hbm, hbm, hbm, hbm, hbm, smem, smem],
        out_specs=(hbm, vmem, vmem),
        scratch_shapes=[
            pltpu.VMEM((2, NV, CA, CT, CR), F32),
            pltpu.VMEM((2 * MAIN, LANES), BF16),
            pltpu.VMEM((parts, VROWS, DROPLETS), F32),
            pltpu.VMEM((LANES, DROPLETS), BF16),
            pltpu.VMEM((8, DROPLETS), jnp.int32),
            pltpu.VMEM((40, DROPLETS), F32),
            pltpu.VMEM((ROWS, DROPLETS), BF16),
            pltpu.VMEM((VROWS, DROPLETS), F32),
            pltpu.VMEM((8, DROPLETS), F32),
            pltpu.VMEM((VROWS, DROPLETS), F32),
            pltpu.VMEM((VROWS, DROPLETS), F32),
            pltpu.VMEM((MAIN + VROWS, LANES), F32),
            pltpu.VMEM((SUBSTEPS, 2, NV, CT, CR), F32),
            pltpu.VMEM((SUBSTEPS, VROWS, LANES), F32),
            pltpu.VMEM((SUBSTEPS, VROWS, LANES), F32),
            pltpu.VMEM((SUBSTEPS, VROWS, LANES), F32),
            pltpu.VMEM((VROWS, LANES), F32),
            pltpu.VMEM((VROWS, LANES), F32),
            pltpu.VMEM((slots, VROWS, BROWS), F32),
            pltpu.VMEM((slots, VROWS, BROWS), F32),
            pltpu.VMEM((NBIN + 1, VROWS, BROWS), F32),
            pltpu.VMEM((CA, CT, CR), F32),
            pltpu.VMEM((NBIN, BROWS), F32),
            pltpu.VMEM((NBIN, BROWS), F32),
            pltpu.VMEM((NBIN, BROWS), jnp.int32),
            pltpu.VMEM((NV, NBIN, BROWS), F32),
            pltpu.SMEM((slots,), jnp.int32),
            sem((6,)), sem((CA,)),
            sem((SUBSTEPS, 2, len(GROUPS))), sem((SUBSTEPS, 2, len(GROUPS))),
            sem((SUBSTEPS, parts)), sem((SUBSTEPS, parts)),
            sem((SUBSTEPS, parts)), sem((SUBSTEPS, parts)),
            sem((SUBSTEPS, parts)), sem((SUBSTEPS, parts)),
            sem((sectors,)), sem((sectors,)),
        ],
        compiler_params=pltpu.CompilerParams(
            collective_id=0, has_side_effects=True, vmem_limit_bytes=62 << 20
        ),
    )(
        gas, diffusivity, swirl, jnp.swapaxes(drops, 0, 1), mass, azim_weight, cell_index, bin_rows,
        destination[:, 0],
    )
    return gas, jnp.swapaxes(moved, 0, 1), rows


def solution(mesh):
    return jax.shard_map(
        body,
        mesh=mesh,
        in_specs=(
            P(None, "axial", "azim", None),
            P(),
            P("axial", "azim", None),
            P(("axial", "azim"), None, None),
            P(("axial", "azim"), None),
            P(("axial", "azim"), None),
            P(("axial", "azim"), None),
            P(("axial", "azim")),
            P(("axial", "azim"), None),
        ),
        out_specs=(
            P(None, "axial", "azim", None),
            P(("axial", "azim"), None, None),
            P(("axial", "azim")),
        ),
        check_vma=False,
    )
```

```python
import functools

import jax
import jax.numpy as jnp
from jax import lax
from jax.experimental import pallas as pl
from jax.experimental.pallas import tpu as pltpu
from jax.sharding import PartitionSpec as P

MESH = pl.DeviceIdType.MESH
F32, BF16 = jnp.float32, jnp.bfloat16

SUBSTEPS = 4
CAP = 2
NV, CA, CT, CR = 13, 8, 32, 128
NBIN, BROWS = 16, 128
DROPLETS = NBIN * BROWS
LANES = CA * CR
MAIN = NV * CT
VROWS = 16
ROWS = 2 * MAIN + 2 * VROWS
HALF = CT // 2
CHUNK = 256

ORDER = (1, 2, 3, 4, 5, 6, 0, 7)
PLACE = {a: i for i, a in enumerate(ORDER)}
PARTS = ((768, 256, (0, 7)), (0, 512, (1, 2, 3, 4)), (512, 256, (5, 6)))
GROUPS = ((0, 5), (5, 4), (9, 4))


def lanes_of(a):
    return pl.ds(PLACE[a] * CR, CR)


def split(x):
    hi = x.astype(BF16)
    return hi, (x - hi.astype(F32)).astype(BF16)


def kernel(
    sectors, slabs,
    gas, diffusivity, swirl, drops, mass, azim_weight, cell_index, bin_rows, destination,
    gas_out, moved_out, rows_out,
    G, F, S, R, WHERE, W, L, D, Q, T, OUT, DEP, AX, LOW, HIGH, DEPR, FIRST, LAST, PAY, GOT, BINS, SW, MASS, WEIGHT, CELL, DROPS, FROM,
    small_sem, save_sem, ax_send, ax_recv, low_send, low_recv, high_send, high_recv, dep_send, dep_recv,
    pay_send, pay_recv,
):
    ax, az = lax.axis_index("axial"), lax.axis_index("azim")
    up_az, down_az = lax.rem(az + 1, sectors), lax.rem(az + sectors - 1, sectors)
    up_ax, down_ax = lax.rem(ax + 1, slabs), lax.rem(ax + slabs - 1, slabs)
    has_up, has_down = ax < slabs - 1, ax > 0

    small = [
        pltpu.make_async_copy(src, dst, small_sem.at[i])
        for i, (src, dst) in enumerate(
            ((mass, MASS), (azim_weight, WEIGHT), (cell_index, CELL), (drops, DROPS), (swirl, SW), (gas, G.at[0]))
        )
    ]

    def axial_of(s, g, layer):
        v0, count = GROUPS[g]
        vs = pl.ds(v0, count)
        upward = pltpu.make_async_remote_copy(
            layer(vs, CA - 1), AX.at[s, 0, vs], ax_send.at[s, 0, g], ax_recv.at[s, 0, g],
            device_id=(up_ax, az), device_id_type=MESH,
        )
        downward = pltpu.make_async_remote_copy(
            layer(vs, 0), AX.at[s, 1, vs], ax_send.at[s, 1, g], ax_recv.at[s, 1, g],
            device_id=(down_ax, az), device_id_type=MESH,
        )
        return upward, downward

    def both(first, first_do, second, second_do):
        @pl.when(first)
        def _():
            first_do()

        @pl.when(second)
        def _():
            second_do()

    def azim_of(s, p):
        lanes = pl.ds(*PARTS[p][:2])
        low = pltpu.make_async_remote_copy(
            LAST.at[:, lanes], LOW.at[s, :, lanes], low_send.at[s, p], low_recv.at[s, p],
            device_id=(ax, up_az), device_id_type=MESH,
        )
        high = pltpu.make_async_remote_copy(
            FIRST.at[:, lanes], HIGH.at[s, :, lanes], high_send.at[s, p], high_recv.at[s, p],
            device_id=(ax, down_az), device_id_type=MESH,
        )
        return low, high

    def dep_of(s, p):
        lanes = pl.ds(*PARTS[p][:2])
        return pltpu.make_async_remote_copy(
            DEP.at[pl.ds(MAIN, VROWS), lanes], DEPR.at[s, :, lanes], dep_send.at[s, p], dep_recv.at[s, p],
            device_id=(ax, up_az), device_id_type=MESH,
        )

    def pay_of(j):
        there = lax.rem(az + j, sectors)
        return pltpu.make_async_remote_copy(
            PAY.at[pl.ds(there * CAP, CAP)], GOT.at[pl.ds(az * CAP, CAP)], pay_send.at[j], pay_recv.at[j],
            device_id=(ax, there), device_id_type=MESH,
        )

    for copy in small:
        copy.start()
    D[...] = jnp.zeros((VROWS, DROPLETS), F32)
    barrier = pltpu.get_barrier_semaphore()
    for j in range(1, sectors):
        pl.semaphore_signal(
            barrier, inc=1, device_id=(ax, lax.rem(az + j, sectors)), device_id_type=MESH
        )
    for other in (up_ax, down_ax):
        pl.semaphore_signal(barrier, inc=1, device_id=(other, az), device_id_type=MESH)

    @pl.when(jnp.logical_not(has_down))
    def _():
        AX[:, 0] = jnp.zeros((SUBSTEPS, NV, CT, CR), F32)

    @pl.when(jnp.logical_not(has_up))
    def _():
        AX[:, 1] = jnp.zeros((SUBSTEPS, NV, CT, CR), F32)

    FIRST[...] = jnp.zeros((VROWS, LANES), F32)
    LAST[...] = jnp.zeros((VROWS, LANES), F32)
    T[...] = jnp.zeros((VROWS, DROPLETS), F32)
    BINS[0] = jnp.zeros((VROWS, BROWS), F32)
    slot = []
    for b in range(NBIN):
        rank = jnp.int32(0)
        for e in range(b):
            rank = rank + jnp.where(destination[e] == destination[b], 1, 0)
        slot.append(destination[b] * CAP + rank)
    for k in range(sectors * CAP):
        source = jnp.int32(0)
        for b in range(NBIN):
            source = source + jnp.where(slot[b] == k, b + 1, 0)
        FROM[k] = source

    for copy in small[:4]:
        copy.wait()
    cell = CELL[...]
    layer = cell // (CT * CR)
    place = jnp.where(layer == 0, CA - 2, jnp.where(layer == CA - 1, CA - 1, layer - 1))
    key = place * CR + cell % CR
    key_row = jnp.concatenate([key[b : b + 1] for b in range(NBIN)], axis=1)
    cell_row = jnp.concatenate([cell[b : b + 1] for b in range(NBIN)], axis=1)
    weight = jnp.concatenate([WEIGHT[b : b + 1, :] for b in range(NBIN)], axis=1)
    m = MASS[...]
    lane = lax.broadcasted_iota(jnp.int32, (1, BROWS), 1)
    half = 0.5 * m / (1.0 + m)
    live = [(lane < bin_rows[b]).astype(F32) for b in range(NBIN)]
    Q[0:1, :] = jnp.concatenate([half[b : b + 1] * live[b] for b in range(NBIN)], axis=1)
    for q in range(2):
        first, count, _ = PARTS[q]
        Q[q + 1 : q + 2, :] = jnp.where(
            key_row >= first, jnp.where(key_row < first + count, 1.0, 0.0), 0.0
        )
    azim_row = cell_row // CR % CT
    WHERE[0:1, :] = cell_row % CR
    WHERE[1:2, :] = cell_row // (CT * CR)
    for t0 in range(0, 40, 8):
        t = lax.broadcasted_iota(jnp.int32, (8, DROPLETS), 0) + t0
        W[t0 : t0 + 8, :] = jnp.where(t == azim_row, 1.0 - weight, 0.0) + jnp.where(
            t == azim_row + 1, weight, 0.0
        )

    @pl.loop(0, LANES // 16)
    def _(k):
        for c in range(0, DROPLETS, 4 * CHUNK):
            rows = lax.broadcasted_iota(jnp.int32, (16, 4 * CHUNK), 0) + k * 16
            R[pl.ds(pl.multiple_of(k * 16, 16), 16), c : c + 4 * CHUNK] = jnp.where(
                rows == key_row[:, c : c + 4 * CHUNK], 1.0, 0.0
            ).astype(BF16)

    pl.semaphore_wait(barrier, sectors + 1)
    for g in range(len(GROUPS)):
        upward, downward = axial_of(0, g, lambda vs, a: gas.at[vs, a])
        both(has_up, upward.start, has_down, downward.start)
    for copy in small[4:]:
        copy.wait()
    for v in range(NV):
        for a in range(CA):
            FIRST[v : v + 1, lanes_of(a)] = G[0, v, a, 0:1, :]
            LAST[v : v + 1, lanes_of(a)] = G[0, v, a, CT - 1 : CT, :]
    for p in range(len(PARTS)):
        for copy in azim_of(0, p):
            copy.start()
    for v in range(NV):
        for a in range(CA):
            hi, lo = split(G[0, v, a])
            F[v * CT : (v + 1) * CT, lanes_of(a)] = hi
            F[MAIN + v * CT : MAIN + (v + 1) * CT, lanes_of(a)] = lo
    for v in range(NV):
        for b in range(NBIN):
            D[v : v + 1, b * BROWS : (b + 1) * BROWS] = DROPS[v, b : b + 1, :]

    def gather_chunk(p, c):
        lanes = pl.ds(*PARTS[p][:2])
        ps = pl.ds(c, CHUNK)
        x = jnp.dot(F[:, lanes], R[lanes, ps], preferred_element_type=F32)
        near = (x[:MAIN] + x[MAIN:]).reshape(NV, CT, CHUNK)
        S[p, 0:NV, ps] = jnp.sum(near * W[0:CT, ps][None], axis=1)

    def gather(p):
        for c in range(0, DROPLETS, CHUNK):
            gather_chunk(p, c)

    def transfers(s, p, beside=None):
        layers = PARTS[p][2]
        for c in range(0, DROPLETS, CHUNK):
            if beside is not None:
                gather_chunk(beside, c)
            ps = pl.ds(c, CHUNK)
            far = []
            for e in range(c, c + CHUNK, BROWS):
                es = pl.ds(e, BROWS)
                at = jnp.broadcast_to(WHERE[0:1, es], (8, BROWS))
                tops = []
                for top in (0, 8):
                    total = jnp.zeros((8, BROWS), F32)
                    for a in layers:
                        value = jnp.take_along_axis(
                            HIGH[s, top : top + 8, lanes_of(a)], at, axis=1, mode="promise_in_bounds"
                        )
                        total = total + jnp.where(WHERE[1:2, es] == a, value, 0.0)
                    tops.append(total)
                far.append(jnp.concatenate(tops, axis=0))
            far = jnp.concatenate(far, axis=1)
            w, w_far = W[0:CT, ps], W[CT : CT + 1, ps]
            sample = S[p, 0:NV, ps] + w_far * far[0:NV]
            rate = Q[0:1, ps] * (1.0 + 0.5 * jnp.tanh(sample[0:1]))
            carried = D[0:NV, ps]
            transfer = rate * (carried - sample)
            if p == 0:
                OUT[0:NV, ps] = transfer
            elif p == 1:
                OUT[0:NV, ps] = jnp.where(Q[1:2, ps] > 0.0, OUT[0:NV, ps], transfer)
            else:
                D[0:NV, ps] = carried - jnp.where(
                    Q[1:2, ps] + Q[2:3, ps] > 0.0, OUT[0:NV, ps], transfer
                )
            twice = 2.0 * transfer
            T[0:NV, ps] = twice
            for v in range(NV):
                hi, lo = split(w * twice[v : v + 1])
                L[p % 2, v * CT : (v + 1) * CT, ps] = hi
                L[p % 2, MAIN + v * CT : MAIN + (v + 1) * CT, ps] = lo
            hi, lo = split(w_far * T[:, ps])
            L[p % 2, 2 * MAIN : 2 * MAIN + VROWS, ps] = hi
            L[p % 2, 2 * MAIN + VROWS : ROWS, ps] = lo

    def deposit(s, p):
        start, width, _ = PARTS[p]
        for k in range(start, start + width, CHUNK):
            ks = pl.ds(k, CHUNK)
            x = lax.dot_general(
                L[p % 2], R[ks, :], (((1,), (1,)), ((), ())), preferred_element_type=F32
            )
            DEP[0:MAIN, ks] = x[:MAIN] + x[MAIN : 2 * MAIN]
            DEP[MAIN : MAIN + VROWS, ks] = x[2 * MAIN : 2 * MAIN + VROWS] + x[2 * MAIN + VROWS :]

    def stencil(s, now, p, halves=(0, 1), vs=(0, NV)):
        later = 1 - now
        sub = lax.broadcasted_iota(jnp.int32, (8, CR), 0)
        column = lax.broadcasted_iota(jnp.int32, (8, CR), 1)
        for v in range(vs[0], vs[0] + vs[1]):
            d = diffusivity[v]
            own = 1.0 - 6.0 * d
            one = pl.ds(v, 1)
            for a in PARTS[p][2]:
                here = lanes_of(a)
                tiles = [G[now, v, a, i * 8 : i * 8 + 8] for i in range(CT // 8)]
                for half in halves:
                    out = []
                    for i in (2 * half, 2 * half + 1):
                        rows = pl.ds(i * 8, 8)
                        c = tiles[i]
                        first = LOW[s, one, here] if i == 0 else pltpu.roll(tiles[i - 1], 1, 0)
                        behind = jnp.where(sub == 0, first, pltpu.roll(c, 1, 0))
                        last = HIGH[s, one, here] if i == 3 else pltpu.roll(tiles[i + 1], 7, 0)
                        ahead = jnp.where(sub == 7, last, pltpu.roll(c, 7, 0))
                        below = AX[s, 0, v, rows] if a == 0 else G[now, v, a - 1, rows]
                        above = AX[s, 1, v, rows] if a == CA - 1 else G[now, v, a + 1, rows]
                        inward = jnp.where(column == 0, 0.0, pltpu.roll(c, 1, 1))
                        outward = jnp.where(column == CR - 1, 0.0, pltpu.roll(c, CR - 1, 1))
                        around = (behind + ahead) + (above + below) + (outward + inward)
                        new = (own * c + d * around) + (SW[a, rows] * (behind - c))
                        new = new + DEP[pl.ds(v * CT + i * 8, 8), here]
                        if i == 0:
                            new = new + jnp.where(sub == 0, DEPR[s, one, here], 0.0)
                            FIRST[one, here] = new[0:1]
                        if i == 3:
                            LAST[one, here] = new[7:8]
                        G[later, v, a, rows] = new
                        out.append(new)
                    hi, lo = split(jnp.concatenate(out, axis=0))
                    at = v * CT + half * 16
                    F[at : at + 16, here] = hi
                    F[MAIN + at : MAIN + at + 16, here] = lo

    def send_bins():
        row = lax.broadcasted_iota(jnp.int32, (VROWS, BROWS), 0)
        for b in range(NBIN):
            alive = (lane < bin_rows[b]).astype(F32)
            BINS[b + 1] = jnp.where(
                row == NV, bin_rows[b].astype(F32), D[:, b * BROWS : (b + 1) * BROWS] * alive
            )
        for k in range(sectors * CAP):
            PAY[k] = BINS[FROM[k]]
        for j in range(1, sectors):
            pay_of(j).start()
        mine = pl.ds(az * CAP, CAP)
        GOT[mine] = PAY[mine]

    def save(a):
        return pltpu.make_async_copy(G.at[SUBSTEPS % 2, :, a], gas_out.at[:, a], save_sem.at[a])

    gather(0)
    gather(1)

    def substep(s, now):
        further = s < SUBSTEPS - 1

        def when_further(do):
            if now == 0:
                do()
            else:
                pl.when(further)(do)

        for p in range(2):
            azim_of(s, p)[1].wait_recv()
        transfers(s, 0, beside=2)
        deposit(s, 0)
        transfers(s, 1)
        dep_of(s, 0).start()
        deposit(s, 1)
        dep_of(s, 1).start()
        azim_of(s, 2)[1].wait_recv()
        transfers(s, 2)
        deposit(s, 2)
        dep_of(s, 2).start()
        if now == 1:
            pl.when(jnp.logical_not(further))(send_bins)
        for p in range(len(PARTS)):
            low, high = azim_of(s, p)
            low.wait_send()
            high.wait_send()
            low.wait_recv()
        dep_of(s, 0).wait_recv()
        for g in range(len(GROUPS)):
            upward, downward = axial_of(s, g, lambda vs, a: G.at[now, vs, a])
            both(has_up, upward.wait_send, has_down, downward.wait_send)
            both(has_down, upward.wait_recv, has_up, downward.wait_recv)
            stencil(s, now, 0, vs=GROUPS[g])

            @when_further
            def _():
                upward, downward = axial_of(s + 1, g, lambda vs, a: G.at[1 - now, vs, a])
                both(has_up, upward.start, has_down, downward.start)

        @when_further
        def _():
            for copy in azim_of(s + 1, 0):
                copy.start()

        def uppers():
            stencil(s, now, 1, (1,))
            stencil(s, now, 2, (1,))

        @when_further
        def _():
            gather(0)
            uppers()

        if now == 1:
            pl.when(jnp.logical_not(further))(uppers)
        dep_of(s, 1).wait_recv()
        stencil(s, now, 1, (0,))

        @when_further
        def _():
            for copy in azim_of(s + 1, 1):
                copy.start()
            gather(1)

        if now == 1:
            @pl.when(jnp.logical_not(further))
            def _():
                for a in PARTS[0][2] + PARTS[1][2]:
                    save(a).start()

        dep_of(s, 2).wait_recv()
        stencil(s, now, 2, (0,))

        @when_further
        def _():
            for copy in azim_of(s + 1, 2):
                copy.start()

        for q in range(len(PARTS)):
            dep_of(s, q).wait_send()

    @pl.loop(0, SUBSTEPS // 2)
    def _(i):
        substep(2 * i, 0)
        substep(2 * i + 1, 1)

    for a in PARTS[2][2]:
        save(a).start()
    for j in range(1, sectors):
        pay_of(j).wait()
    lines = jnp.concatenate([GOT[k, NV : NV + 1, :] for k in range(sectors * CAP)], axis=0)
    at = lax.broadcasted_iota(jnp.int32, lines.shape, 0)
    column = lax.broadcasted_iota(jnp.int32, lines.shape, 1)
    counts = jnp.sum(jnp.where(at == column, lines, 0.0), axis=0)
    rows_out[...] = counts[: sectors * CAP].astype(jnp.int32)
    for k in range(sectors * CAP):
        for v in range(NV):
            moved_out[v, k : k + 1, :] = GOT[k, v : v + 1, :]
    for a in range(CA):
        save(a).wait()


def body(gas, diffusivity, swirl, drops, mass, azim_weight, cell_index, bin_rows, destination):
    sectors, slabs = lax.axis_size("azim"), lax.axis_size("axial")
    hbm = pl.BlockSpec(memory_space=pltpu.HBM)
    vmem = pl.BlockSpec(memory_space=pltpu.VMEM)
    smem = pl.BlockSpec(memory_space=pltpu.SMEM)
    sem = pltpu.SemaphoreType.DMA
    parts = len(PARTS)
    slots = sectors * CAP
    gas, moved, rows = pl.pallas_call(
        functools.partial(kernel, sectors, slabs),
        out_shape=(
            jax.ShapeDtypeStruct((NV, CA, CT, CR), F32),
            jax.ShapeDtypeStruct((NV, slots, BROWS), F32),
            jax.ShapeDtypeStruct((slots,), jnp.int32),
        ),
        in_specs=[hbm, smem, hbm, hbm, hbm, hbm, hbm, smem, smem],
        out_specs=(hbm, vmem, vmem),
        scratch_shapes=[
            pltpu.VMEM((2, NV, CA, CT, CR), F32),
            pltpu.VMEM((2 * MAIN, LANES), BF16),
            pltpu.VMEM((parts, VROWS, DROPLETS), F32),
            pltpu.VMEM((LANES, DROPLETS), BF16),
            pltpu.VMEM((8, DROPLETS), jnp.int32),
            pltpu.VMEM((40, DROPLETS), F32),
            pltpu.VMEM((2, ROWS, DROPLETS), BF16),
            pltpu.VMEM((VROWS, DROPLETS), F32),
            pltpu.VMEM((8, DROPLETS), F32),
            pltpu.VMEM((VROWS, DROPLETS), F32),
            pltpu.VMEM((VROWS, DROPLETS), F32),
            pltpu.VMEM((MAIN + VROWS, LANES), F32),
            pltpu.VMEM((SUBSTEPS, 2, NV, CT, CR), F32),
            pltpu.VMEM((SUBSTEPS, VROWS, LANES), F32),
            pltpu.VMEM((SUBSTEPS, VROWS, LANES), F32),
            pltpu.VMEM((SUBSTEPS, VROWS, LANES), F32),
            pltpu.VMEM((VROWS, LANES), F32),
            pltpu.VMEM((VROWS, LANES), F32),
            pltpu.VMEM((slots, VROWS, BROWS), F32),
            pltpu.VMEM((slots, VROWS, BROWS), F32),
            pltpu.VMEM((NBIN + 1, VROWS, BROWS), F32),
            pltpu.VMEM((CA, CT, CR), F32),
            pltpu.VMEM((NBIN, BROWS), F32),
            pltpu.VMEM((NBIN, BROWS), F32),
            pltpu.VMEM((NBIN, BROWS), jnp.int32),
            pltpu.VMEM((NV, NBIN, BROWS), F32),
            pltpu.SMEM((slots,), jnp.int32),
            sem((6,)), sem((CA,)),
            sem((SUBSTEPS, 2, len(GROUPS))), sem((SUBSTEPS, 2, len(GROUPS))),
            sem((SUBSTEPS, parts)), sem((SUBSTEPS, parts)),
            sem((SUBSTEPS, parts)), sem((SUBSTEPS, parts)),
            sem((SUBSTEPS, parts)), sem((SUBSTEPS, parts)),
            sem((sectors,)), sem((sectors,)),
        ],
        compiler_params=pltpu.CompilerParams(
            collective_id=0, has_side_effects=True, vmem_limit_bytes=62 << 20
        ),
    )(
        gas, diffusivity, swirl, jnp.swapaxes(drops, 0, 1), mass, azim_weight, cell_index, bin_rows,
        destination[:, 0],
    )
    return gas, jnp.swapaxes(moved, 0, 1), rows


def solution(mesh):
    return jax.shard_map(
        body,
        mesh=mesh,
        in_specs=(
            P(None, "axial", "azim", None),
            P(),
            P("axial", "azim", None),
            P(("axial", "azim"), None, None),
            P(("axial", "azim"), None),
            P(("axial", "azim"), None),
            P(("axial", "azim"), None),
            P(("axial", "azim")),
            P(("axial", "azim"), None),
        ),
        out_specs=(
            P(None, "axial", "azim", None),
            P(("axial", "azim"), None, None),
            P(("axial", "azim")),
        ),
        check_vma=False,
    )
```

```python
import functools

import jax
import jax.numpy as jnp
from jax import lax
from jax.experimental import pallas as pl
from jax.experimental.pallas import tpu as pltpu
from jax.sharding import PartitionSpec as P

MESH = pl.DeviceIdType.MESH
F32, BF16 = jnp.float32, jnp.bfloat16

SUBSTEPS = 4
CAP = 2
NV, CA, CT, CR = 13, 8, 32, 128
NBIN, BROWS = 16, 128
DROPLETS = NBIN * BROWS
LANES = CA * CR
MAIN = NV * CT
VROWS = 16
ROWS = 2 * MAIN + 2 * VROWS
HALF = CT // 2
CHUNK = 256

ORDER = (1, 2, 3, 4, 5, 6, 0, 7)
PLACE = {a: i for i, a in enumerate(ORDER)}
PARTS = ((768, 256, (0, 7)), (0, 512, (1, 2, 3, 4)), (512, 256, (5, 6)))
GROUPS = ((0, 5), (5, 4), (9, 4))


def lanes_of(a):
    return pl.ds(PLACE[a] * CR, CR)


def split(x):
    hi = x.astype(BF16)
    return hi, (x - hi.astype(F32)).astype(BF16)


def kernel(
    sectors, slabs,
    gas, diffusivity, swirl, drops, mass, azim_weight, cell_index, bin_rows, destination,
    gas_out, moved_out, rows_out,
    G, F, S, R, WHERE, W, L, D, Q, T, OUT, DEP, AX, LOW, HIGH, DEPR, FIRST, LAST, PAY, GOT, BINS, SW, MASS, WEIGHT, CELL, DROPS, FROM,
    small_sem, save_sem, ax_send, ax_recv, low_send, low_recv, high_send, high_recv, dep_send, dep_recv,
    pay_send, pay_recv,
):
    ax, az = lax.axis_index("axial"), lax.axis_index("azim")
    up_az, down_az = lax.rem(az + 1, sectors), lax.rem(az + sectors - 1, sectors)
    up_ax, down_ax = lax.rem(ax + 1, slabs), lax.rem(ax + slabs - 1, slabs)
    low_on, high_on = jnp.where(ax > 0, 1.0, 0.0), jnp.where(ax < slabs - 1, 1.0, 0.0)

    small = [
        pltpu.make_async_copy(src, dst, small_sem.at[i])
        for i, (src, dst) in enumerate(
            ((mass, MASS), (azim_weight, WEIGHT), (cell_index, CELL), (drops, DROPS), (swirl, SW), (gas, G.at[0]))
        )
    ]

    def axial_of(s, g, layer):
        v0, count = GROUPS[g]
        vs = pl.ds(v0, count)
        upward = pltpu.make_async_remote_copy(
            layer(vs, CA - 1), AX.at[s, 0, vs], ax_send.at[s, 0, g], ax_recv.at[s, 0, g],
            device_id=(up_ax, az), device_id_type=MESH,
        )
        downward = pltpu.make_async_remote_copy(
            layer(vs, 0), AX.at[s, 1, vs], ax_send.at[s, 1, g], ax_recv.at[s, 1, g],
            device_id=(down_ax, az), device_id_type=MESH,
        )
        return upward, downward

    def azim_of(s, p):
        lanes = pl.ds(*PARTS[p][:2])
        low = pltpu.make_async_remote_copy(
            LAST.at[:, lanes], LOW.at[s, :, lanes], low_send.at[s, p], low_recv.at[s, p],
            device_id=(ax, up_az), device_id_type=MESH,
        )
        high = pltpu.make_async_remote_copy(
            FIRST.at[:, lanes], HIGH.at[s, :, lanes], high_send.at[s, p], high_recv.at[s, p],
            device_id=(ax, down_az), device_id_type=MESH,
        )
        return low, high

    def dep_of(s, p):
        lanes = pl.ds(*PARTS[p][:2])
        return pltpu.make_async_remote_copy(
            DEP.at[pl.ds(MAIN, VROWS), lanes], DEPR.at[s, :, lanes], dep_send.at[s, p], dep_recv.at[s, p],
            device_id=(ax, up_az), device_id_type=MESH,
        )

    def pay_of(j):
        there = lax.rem(az + j, sectors)
        return pltpu.make_async_remote_copy(
            PAY.at[pl.ds(there * CAP, CAP)], GOT.at[pl.ds(az * CAP, CAP)], pay_send.at[j], pay_recv.at[j],
            device_id=(ax, there), device_id_type=MESH,
        )

    for copy in small:
        copy.start()
    D[...] = jnp.zeros((VROWS, DROPLETS), F32)
    barrier = pltpu.get_barrier_semaphore()
    for j in range(1, sectors):
        pl.semaphore_signal(
            barrier, inc=1, device_id=(ax, lax.rem(az + j, sectors)), device_id_type=MESH
        )
    for other in (up_ax, down_ax):
        pl.semaphore_signal(barrier, inc=1, device_id=(other, az), device_id_type=MESH)

    FIRST[...] = jnp.zeros((VROWS, LANES), F32)
    LAST[...] = jnp.zeros((VROWS, LANES), F32)
    T[...] = jnp.zeros((VROWS, DROPLETS), F32)
    BINS[0] = jnp.zeros((VROWS, BROWS), F32)
    slot = []
    for b in range(NBIN):
        rank = jnp.int32(0)
        for e in range(b):
            rank = rank + jnp.where(destination[e] == destination[b], 1, 0)
        slot.append(destination[b] * CAP + rank)
    for k in range(sectors * CAP):
        source = jnp.int32(0)
        for b in range(NBIN):
            source = source + jnp.where(slot[b] == k, b + 1, 0)
        FROM[k] = source

    for copy in small[:4]:
        copy.wait()
    cell = CELL[...]
    layer = cell // (CT * CR)
    place = jnp.where(layer == 0, CA - 2, jnp.where(layer == CA - 1, CA - 1, layer - 1))
    key = place * CR + cell % CR
    key_row = jnp.concatenate([key[b : b + 1] for b in range(NBIN)], axis=1)
    cell_row = jnp.concatenate([cell[b : b + 1] for b in range(NBIN)], axis=1)
    weight = jnp.concatenate([WEIGHT[b : b + 1, :] for b in range(NBIN)], axis=1)
    m = MASS[...]
    lane = lax.broadcasted_iota(jnp.int32, (1, BROWS), 1)
    half = 0.5 * m / (1.0 + m)
    live = [(lane < bin_rows[b]).astype(F32) for b in range(NBIN)]
    Q[0:1, :] = jnp.concatenate([half[b : b + 1] * live[b] for b in range(NBIN)], axis=1)
    for q in range(2):
        first, count, _ = PARTS[q]
        Q[q + 1 : q + 2, :] = jnp.where(
            key_row >= first, jnp.where(key_row < first + count, 1.0, 0.0), 0.0
        )
    azim_row = cell_row // CR % CT
    WHERE[0:1, :] = cell_row % CR
    WHERE[1:2, :] = cell_row // (CT * CR)
    for t0 in range(0, 40, 8):
        t = lax.broadcasted_iota(jnp.int32, (8, DROPLETS), 0) + t0
        W[t0 : t0 + 8, :] = jnp.where(t == azim_row, 1.0 - weight, 0.0) + jnp.where(
            t == azim_row + 1, weight, 0.0
        )

    def one_hot(k):
        for c in range(0, DROPLETS, 4 * CHUNK):
            rows = lax.broadcasted_iota(jnp.int32, (16, 4 * CHUNK), 0) + k * 16
            R[pl.ds(pl.multiple_of(k * 16, 16), 16), c : c + 4 * CHUNK] = jnp.where(
                rows == key_row[:, c : c + 4 * CHUNK], 1.0, 0.0
            ).astype(BF16)

    pl.loop(0, LANES // 32)(one_hot)
    pl.semaphore_wait(barrier, sectors + 1)
    for g in range(len(GROUPS)):
        for copy in axial_of(0, g, lambda vs, a: gas.at[vs, a]):
            copy.start()
    pl.loop(LANES // 32, LANES // 16)(one_hot)
    for copy in small[4:]:
        copy.wait()
    for v in range(NV):
        for a in range(CA):
            FIRST[v : v + 1, lanes_of(a)] = G[0, v, a, 0:1, :]
            LAST[v : v + 1, lanes_of(a)] = G[0, v, a, CT - 1 : CT, :]
    for p in range(len(PARTS)):
        for copy in azim_of(0, p):
            copy.start()
    for v in range(NV):
        for a in range(CA):
            hi, lo = split(G[0, v, a])
            F[v * CT : (v + 1) * CT, lanes_of(a)] = hi
            F[MAIN + v * CT : MAIN + (v + 1) * CT, lanes_of(a)] = lo
    for v in range(NV):
        for b in range(NBIN):
            D[v : v + 1, b * BROWS : (b + 1) * BROWS] = DROPS[v, b : b + 1, :]

    def gather_chunk(p, c):
        lanes = pl.ds(*PARTS[p][:2])
        ps = pl.ds(c, CHUNK)
        x = jnp.dot(F[:, lanes], R[lanes, ps], preferred_element_type=F32)
        near = (x[:MAIN] + x[MAIN:]).reshape(NV, CT, CHUNK)
        S[p, 0:NV, ps] = jnp.sum(near * W[0:CT, ps][None], axis=1)

    def gather(p):
        for c in range(0, DROPLETS, CHUNK):
            gather_chunk(p, c)

    def transfers(s, p, beside=None):
        layers = PARTS[p][2]
        for c in range(0, DROPLETS, CHUNK):
            if beside is not None:
                gather_chunk(beside, c)
            ps = pl.ds(c, CHUNK)
            far = []
            for e in range(c, c + CHUNK, BROWS):
                es = pl.ds(e, BROWS)
                at = jnp.broadcast_to(WHERE[0:1, es], (8, BROWS))
                tops = []
                for top in (0, 8):
                    total = jnp.zeros((8, BROWS), F32)
                    for a in layers:
                        value = jnp.take_along_axis(
                            HIGH[s, top : top + 8, lanes_of(a)], at, axis=1, mode="promise_in_bounds"
                        )
                        total = total + jnp.where(WHERE[1:2, es] == a, value, 0.0)
                    tops.append(total)
                far.append(jnp.concatenate(tops, axis=0))
            far = jnp.concatenate(far, axis=1)
            w, w_far = W[0:CT, ps], W[CT : CT + 1, ps]
            sample = S[p, 0:NV, ps] + w_far * far[0:NV]
            rate = Q[0:1, ps] * (1.0 + 0.5 * jnp.tanh(sample[0:1]))
            carried = D[0:NV, ps]
            transfer = rate * (carried - sample)
            if p == 0:
                OUT[0:NV, ps] = transfer
            elif p == 1:
                OUT[0:NV, ps] = jnp.where(Q[1:2, ps] > 0.0, OUT[0:NV, ps], transfer)
            else:
                D[0:NV, ps] = carried - jnp.where(
                    Q[1:2, ps] + Q[2:3, ps] > 0.0, OUT[0:NV, ps], transfer
                )
            twice = 2.0 * transfer
            T[0:NV, ps] = twice
            for v in range(NV):
                hi, lo = split(w * twice[v : v + 1])
                L[p % 2, v * CT : (v + 1) * CT, ps] = hi
                L[p % 2, MAIN + v * CT : MAIN + (v + 1) * CT, ps] = lo
            hi, lo = split(w_far * T[:, ps])
            L[p % 2, 2 * MAIN : 2 * MAIN + VROWS, ps] = hi
            L[p % 2, 2 * MAIN + VROWS : ROWS, ps] = lo

    def deposit(s, p):
        start, width, _ = PARTS[p]
        for k in range(start, start + width, CHUNK):
            ks = pl.ds(k, CHUNK)
            x = lax.dot_general(
                L[p % 2], R[ks, :], (((1,), (1,)), ((), ())), preferred_element_type=F32
            )
            DEP[0:MAIN, ks] = x[:MAIN] + x[MAIN : 2 * MAIN]
            DEP[MAIN : MAIN + VROWS, ks] = x[2 * MAIN : 2 * MAIN + VROWS] + x[2 * MAIN + VROWS :]

    def stencil(s, now, p, halves=(0, 1), vs=(0, NV)):
        later = 1 - now
        sub = lax.broadcasted_iota(jnp.int32, (8, CR), 0)
        column = lax.broadcasted_iota(jnp.int32, (8, CR), 1)
        for v in range(vs[0], vs[0] + vs[1]):
            d = diffusivity[v]
            own = 1.0 - 6.0 * d
            one = pl.ds(v, 1)
            for a in PARTS[p][2]:
                here = lanes_of(a)
                tiles = [G[now, v, a, i * 8 : i * 8 + 8] for i in range(CT // 8)]
                for half in halves:
                    out = []
                    for i in (2 * half, 2 * half + 1):
                        rows = pl.ds(i * 8, 8)
                        c = tiles[i]
                        first = LOW[s, one, here] if i == 0 else pltpu.roll(tiles[i - 1], 1, 0)
                        behind = jnp.where(sub == 0, first, pltpu.roll(c, 1, 0))
                        last = HIGH[s, one, here] if i == 3 else pltpu.roll(tiles[i + 1], 7, 0)
                        ahead = jnp.where(sub == 7, last, pltpu.roll(c, 7, 0))
                        below = AX[s, 0, v, rows] * low_on if a == 0 else G[now, v, a - 1, rows]
                        above = AX[s, 1, v, rows] * high_on if a == CA - 1 else G[now, v, a + 1, rows]
                        inward = jnp.where(column == 0, 0.0, pltpu.roll(c, 1, 1))
                        outward = jnp.where(column == CR - 1, 0.0, pltpu.roll(c, CR - 1, 1))
                        around = (behind + ahead) + (above + below) + (outward + inward)
                        new = (own * c + d * around) + (SW[a, rows] * (behind - c))
                        new = new + DEP[pl.ds(v * CT + i * 8, 8), here]
                        if i == 0:
                            new = new + jnp.where(sub == 0, DEPR[s, one, here], 0.0)
                            FIRST[one, here] = new[0:1]
                        if i == 3:
                            LAST[one, here] = new[7:8]
                        G[later, v, a, rows] = new
                        out.append(new)
                    hi, lo = split(jnp.concatenate(out, axis=0))
                    at = v * CT + half * 16
                    F[at : at + 16, here] = hi
                    F[MAIN + at : MAIN + at + 16, here] = lo

    def send_bins():
        row = lax.broadcasted_iota(jnp.int32, (VROWS, BROWS), 0)
        for b in range(NBIN):
            alive = (lane < bin_rows[b]).astype(F32)
            BINS[b + 1] = jnp.where(
                row == NV, bin_rows[b].astype(F32), D[:, b * BROWS : (b + 1) * BROWS] * alive
            )
        for k in range(sectors * CAP):
            PAY[k] = BINS[FROM[k]]
        for j in range(1, sectors):
            pay_of(j).start()
        mine = pl.ds(az * CAP, CAP)
        GOT[mine] = PAY[mine]

    def save(a):
        return pltpu.make_async_copy(G.at[SUBSTEPS % 2, :, a], gas_out.at[:, a], save_sem.at[a])

    gather(0)
    gather(1)

    def substep(s, now):
        further = s < SUBSTEPS - 1

        def when_further(do):
            if now == 0:
                do()
            else:
                pl.when(further)(do)

        for p in range(2):
            azim_of(s, p)[1].wait_recv()
        transfers(s, 0, beside=2)
        deposit(s, 0)
        transfers(s, 1)
        dep_of(s, 0).start()
        deposit(s, 1)
        dep_of(s, 1).start()
        azim_of(s, 2)[1].wait_recv()
        transfers(s, 2)
        deposit(s, 2)
        dep_of(s, 2).start()
        if now == 1:
            pl.when(jnp.logical_not(further))(send_bins)
        for p in range(len(PARTS)):
            low, high = azim_of(s, p)
            low.wait_send()
            high.wait_send()
            low.wait_recv()
        dep_of(s, 0).wait_recv()
        for g in range(len(GROUPS)):
            for copy in axial_of(s, g, lambda vs, a: G.at[now, vs, a]):
                copy.wait()
            stencil(s, now, 0, vs=GROUPS[g])

            @when_further
            def _():
                for copy in axial_of(s + 1, g, lambda vs, a: G.at[1 - now, vs, a]):
                    copy.start()

        @when_further
        def _():
            for copy in azim_of(s + 1, 0):
                copy.start()

        def uppers():
            stencil(s, now, 1, (1,))
            stencil(s, now, 2, (1,))

        @when_further
        def _():
            gather(0)
            uppers()

        if now == 1:
            pl.when(jnp.logical_not(further))(uppers)
        dep_of(s, 1).wait_recv()
        stencil(s, now, 1, (0,))

        @when_further
        def _():
            for copy in azim_of(s + 1, 1):
                copy.start()
            gather(1)

        if now == 1:
            @pl.when(jnp.logical_not(further))
            def _():
                for a in PARTS[0][2] + PARTS[1][2]:
                    save(a).start()

        dep_of(s, 2).wait_recv()
        stencil(s, now, 2, (0,))

        @when_further
        def _():
            for copy in azim_of(s + 1, 2):
                copy.start()

        for q in range(len(PARTS)):
            dep_of(s, q).wait_send()

    @pl.loop(0, SUBSTEPS // 2)
    def _(i):
        substep(2 * i, 0)
        substep(2 * i + 1, 1)

    for a in PARTS[2][2]:
        save(a).start()
    for j in range(1, sectors):
        pay_of(j).wait()
    lines = jnp.concatenate([GOT[k, NV : NV + 1, :] for k in range(sectors * CAP)], axis=0)
    at = lax.broadcasted_iota(jnp.int32, lines.shape, 0)
    column = lax.broadcasted_iota(jnp.int32, lines.shape, 1)
    counts = jnp.sum(jnp.where(at == column, lines, 0.0), axis=0)
    rows_out[...] = counts[: sectors * CAP].astype(jnp.int32)
    for k in range(sectors * CAP):
        for v in range(NV):
            moved_out[v, k : k + 1, :] = GOT[k, v : v + 1, :]
    for a in range(CA):
        save(a).wait()


def body(gas, diffusivity, swirl, drops, mass, azim_weight, cell_index, bin_rows, destination):
    sectors, slabs = lax.axis_size("azim"), lax.axis_size("axial")
    hbm = pl.BlockSpec(memory_space=pltpu.HBM)
    vmem = pl.BlockSpec(memory_space=pltpu.VMEM)
    smem = pl.BlockSpec(memory_space=pltpu.SMEM)
    sem = pltpu.SemaphoreType.DMA
    parts = len(PARTS)
    slots = sectors * CAP
    gas, moved, rows = pl.pallas_call(
        functools.partial(kernel, sectors, slabs),
        out_shape=(
            jax.ShapeDtypeStruct((NV, CA, CT, CR), F32),
            jax.ShapeDtypeStruct((NV, slots, BROWS), F32),
            jax.ShapeDtypeStruct((slots,), jnp.int32),
        ),
        in_specs=[hbm, smem, hbm, hbm, hbm, hbm, hbm, smem, smem],
        out_specs=(hbm, vmem, vmem),
        scratch_shapes=[
            pltpu.VMEM((2, NV, CA, CT, CR), F32),
            pltpu.VMEM((2 * MAIN, LANES), BF16),
            pltpu.VMEM((parts, VROWS, DROPLETS), F32),
            pltpu.VMEM((LANES, DROPLETS), BF16),
            pltpu.VMEM((8, DROPLETS), jnp.int32),
            pltpu.VMEM((40, DROPLETS), F32),
            pltpu.VMEM((2, ROWS, DROPLETS), BF16),
            pltpu.VMEM((VROWS, DROPLETS), F32),
            pltpu.VMEM((8, DROPLETS), F32),
            pltpu.VMEM((VROWS, DROPLETS), F32),
            pltpu.VMEM((VROWS, DROPLETS), F32),
            pltpu.VMEM((MAIN + VROWS, LANES), F32),
            pltpu.VMEM((SUBSTEPS, 2, NV, CT, CR), F32),
            pltpu.VMEM((SUBSTEPS, VROWS, LANES), F32),
            pltpu.VMEM((SUBSTEPS, VROWS, LANES), F32),
            pltpu.VMEM((SUBSTEPS, VROWS, LANES), F32),
            pltpu.VMEM((VROWS, LANES), F32),
            pltpu.VMEM((VROWS, LANES), F32),
            pltpu.VMEM((slots, VROWS, BROWS), F32),
            pltpu.VMEM((slots, VROWS, BROWS), F32),
            pltpu.VMEM((NBIN + 1, VROWS, BROWS), F32),
            pltpu.VMEM((CA, CT, CR), F32),
            pltpu.VMEM((NBIN, BROWS), F32),
            pltpu.VMEM((NBIN, BROWS), F32),
            pltpu.VMEM((NBIN, BROWS), jnp.int32),
            pltpu.VMEM((NV, NBIN, BROWS), F32),
            pltpu.SMEM((slots,), jnp.int32),
            sem((6,)), sem((CA,)),
            sem((SUBSTEPS, 2, len(GROUPS))), sem((SUBSTEPS, 2, len(GROUPS))),
            sem((SUBSTEPS, parts)), sem((SUBSTEPS, parts)),
            sem((SUBSTEPS, parts)), sem((SUBSTEPS, parts)),
            sem((SUBSTEPS, parts)), sem((SUBSTEPS, parts)),
            sem((sectors,)), sem((sectors,)),
        ],
        compiler_params=pltpu.CompilerParams(
            collective_id=0, has_side_effects=True, vmem_limit_bytes=62 << 20
        ),
    )(
        gas, diffusivity, swirl, jnp.swapaxes(drops, 0, 1), mass, azim_weight, cell_index, bin_rows,
        destination[:, 0],
    )
    return gas, jnp.swapaxes(moved, 0, 1), rows


def solution(mesh):
    return jax.shard_map(
        body,
        mesh=mesh,
        in_specs=(
            P(None, "axial", "azim", None),
            P(),
            P("axial", "azim", None),
            P(("axial", "azim"), None, None),
            P(("axial", "azim"), None),
            P(("axial", "azim"), None),
            P(("axial", "azim"), None),
            P(("axial", "azim")),
            P(("axial", "azim"), None),
        ),
        out_specs=(
            P(None, "axial", "azim", None),
            P(("axial", "azim"), None, None),
            P(("axial", "azim")),
        ),
        check_vma=False,
    )
```
